32 devices in a mesh: grp: 2 (over y), view: 8 (over z, x), frame: 2 (over core).
Axes of the slice: x: 2, y: 2, z: 4, core: 2. Of those that a mesh axis runs over, the one named last changes fastest.
Arguments:
- sinogram: float32 [32, 128], P(('grp', 'frame'), 'view'), parts along dimension 0, may hold values from -6 to 6
- stat_weight: float32 [32, 128], P(('grp', 'frame'), 'view'), parts along dimension 0, may hold values from 0.5 to 2
- projector: bfloat16 [128, 230400], P('view'), may hold values from -0.0234375 to 0.0234375
- block_mask: int32 [8, 64], P('view'), may hold values 0 or 1
- kinetic: float32 [2, 460800], P(None, ('grp', 'view', 'frame')), parts along dimension 1, may hold values from 0 to 1
- curvature: float32 [16, 460800], P(None, ('grp', 'view', 'frame')), parts along dimension 1, may hold values from 0.02 to 0.2
- plasma: float32 [7200], P('grp'), parts along dimension 0, may hold values from 0.25 to 8, as said below
- bounds: int32 [34], P('grp'), parts along dimension 0, may hold values from 900 to 3600, as said below
Outputs:
- kinetic_new: float32 [2, 460800], P(None, ('grp', 'view', 'frame')), parts along dimension 1
The draws below stay inside these ranges and needn't reach their ends.
There are 2 independent parts, one for each index of `grp`. The reference program is written for one: setup_inputs(seed, part) draws one part's arguments, and reference() takes and returns one part's arrays. A program takes and returns all parts, laid end to end along the dimension named above; an argument that names none is the same for every part. Nothing has to cross between parts.
Inputs may be any that keep to these rules, and one draw needn't show every extreme that they name: `bounds`: strictly increasing frame boundaries; the first is 900 and the last 3600. Positive plasma activity.
All inputs are finite; a program needn't handle non-finite values. No bound on the sum of `block_mask` on one device may be relied on, other than what follows from the above.
Results may differ from the reference program's by a relative error of at most 0.0038.
Values sent between devices are 32-bit elements; how exact they have to be, the bound alone decides.
A program may use at most 256 MiB of HBM per device.

```python
import math
import jax
import jax.numpy as jnp
from jax import lax

NVOX = 230400
NVB = 64
BINS_DEV = 16
BINS = 128
FRAMES = 16
TSAMP = 3600
N_VIEW = 8


def draw_plasma(key, part):
    key = jax.random.fold_in(key, 11)
    subkeys = jax.random.split(key, 4)
    seconds = jnp.arange(TSAMP, dtype=jnp.float32)
    decay_time = TSAMP * jax.random.uniform(subkeys[0], (), jnp.float32, 0.05, 0.2)
    amplitude = jax.random.uniform(subkeys[1], (), jnp.float32, 4.0, 8.0)
    baseline = jax.random.uniform(subkeys[2], (), jnp.float32, 0.2, 0.5)
    roughness = jnp.exp(jax.random.uniform(subkeys[3], (TSAMP,), jnp.float32, math.log(0.4), math.log(2.5)))
    profile = (baseline + amplitude * jnp.exp(-seconds / decay_time)) * roughness
    return jnp.clip(profile, 0.25, 8.0)


def draw_bounds(key, part):
    key = jax.random.fold_in(key, 23)
    opening = TSAMP // 4
    interior = TSAMP - opening - 1
    chosen = jax.random.permutation(key, interior)[:FRAMES - 1] + opening + 1
    interior_marks = jnp.sort(chosen).astype(jnp.int32)
    return jnp.concatenate([jnp.array([opening], jnp.int32), interior_marks, jnp.array([TSAMP], jnp.int32)])


def set_ends(entries, own_key, least, largest):
    extent = entries.shape
    place = [jax.random.randint(jax.random.fold_in(own_key, axis), (), 0, extent[axis]) for axis in range(len(extent))]
    entries = entries.at[tuple(place)].set(least)
    longest = extent.index(max(extent))
    place[longest] = (place[longest] + 1) % extent[longest]
    return entries.at[tuple(place)].set(largest)


def raised(result, stream_key, source, target, blocks, factor):
    owner, partner = [(jnp.arange(result.shape[position]) // (result.shape[position] // blocks)).reshape([-1 if axis == position else 1 for axis in range(result.ndim)]) for position in (source, target)]
    chosen = jax.random.permutation(stream_key, blocks)[partner]
    strong = (owner == chosen) | (owner == (partner + blocks // 2) % blocks)
    return jnp.where(strong, factor * result, result)


def block_scale(own_key, extent, cuts, least, largest):
    def one(position, blocks):
        draws = jax.random.uniform(jax.random.fold_in(jax.random.fold_in(own_key, 6), position), (blocks,), jnp.float32, least / len(cuts), largest / len(cuts))
        return jnp.repeat(jnp.exp(draws), extent[position] // blocks).reshape((-1,) + (1,) * (len(extent) - position - 1))

    factor_of = one(*cuts[0])
    for cut in cuts[1:]:
        factor_of = factor_of * one(*cut)
    return factor_of


def bell_draw(own_key, extent, spread, reach, shards=(), kind=jnp.bfloat16):
    values = jax.random.normal(own_key, extent, jnp.float32) * spread
    if len(shards) > 0:
        values = block_scale(own_key, extent, shards, -0.22, 0.18) * values
    return jnp.clip(values, min=-reach, max=reach).astype(kind)


def gaussian_with(rng, dims, deviation, limit, cuts, heavy, kind=jnp.bfloat16):
    drawn = deviation * jax.random.normal(rng, dims, jnp.float32)
    if cuts:
        drawn = drawn * block_scale(rng, dims, cuts, -0.22, 0.18)
    return jnp.clip(raised(drawn, jax.random.fold_in(rng, 3), *heavy), -limit, limit).astype(kind)


def setup_inputs(seed: int = 0, part: int = 0) -> dict:
    arg_keys = jax.random.split(jax.random.key(seed), 9)
    own_keys = jax.random.split(jax.random.fold_in(arg_keys[8], part), 9)
    sinogram = bell_draw(own_keys[0], (FRAMES, BINS), 1.0, 6.0, ((0, 2), (1, 8)), jnp.float32)
    stat_weight = jnp.clip(jnp.exp(math.log(2.0) - 1.3862944 * jax.random.uniform(own_keys[1], (FRAMES, BINS), jnp.float32) ** block_scale(own_keys[1], (FRAMES, BINS), ((0, 2), (1, 8)), -0.2, 0.2)), 0.5, 2.0)
    projector = gaussian_with(arg_keys[2], (BINS, NVOX), (NVOX // 2) ** -0.5, 0.0234375, ((0, 8),), (0, 1, 8, 2.0))
    block_mask = set_ends((jax.random.randint(arg_keys[3], (N_VIEW, NVB), 0, 2) < 1).astype(jnp.int32), jax.random.fold_in(arg_keys[3], 1), 0, 1)
    kinetic = jnp.clip(1.0 * jax.random.uniform(own_keys[4], (2, NVOX), jnp.float32) ** block_scale(own_keys[4], (2, NVOX), ((1, 16),), -0.2, 0.2), 0.0, 1.0)
    curvature = jnp.clip(jnp.exp(math.log(0.2) - 2.3025851 * jax.random.uniform(own_keys[5], (FRAMES, NVOX), jnp.float32) ** block_scale(own_keys[5], (FRAMES, NVOX), ((1, 16),), -0.2, 0.2)), 0.02, 0.2)
    plasma = draw_plasma(jax.random.fold_in(jax.random.fold_in(arg_keys[8], part), 71), part)
    bounds = draw_bounds(jax.random.fold_in(jax.random.fold_in(arg_keys[8], part), 71), part)
    return {"sinogram": sinogram, "stat_weight": stat_weight, "projector": projector, "block_mask": block_mask, "kinetic": kinetic, "curvature": curvature, "plasma": plasma, "bounds": bounds}


def frame_tables(bounds, plasma):
    starts = bounds[:-1]
    finish = bounds[1:]
    seconds = jnp.arange(plasma.shape[0], dtype=jnp.int32)
    inside = ((seconds[None, :] >= starts[:, None]) & (seconds[None, :] < finish[:, None])).astype(jnp.float32)
    reaches = jnp.clip(finish[:, None] - jnp.maximum(seconds[None, :], starts[:, None]), 0).astype(jnp.float32)
    length = (finish - starts).astype(jnp.float32)
    plasma_mean = jnp.dot(inside, plasma, precision=lax.Precision.HIGHEST) / length
    integral = jnp.dot(reaches, plasma, precision=lax.Precision.HIGHEST) / (length * plasma.shape[0])
    return integral, plasma_mean


def fit_kinetic(curvature, integral, plasma_mean, rhs_slope, rhs_inter):
    coef_cc = jnp.sum(curvature * (integral * integral)[:, None], axis=0)
    coef_cp = jnp.sum(curvature * (integral * plasma_mean)[:, None], axis=0)
    coef_pp = jnp.sum(curvature * (plasma_mean * plasma_mean)[:, None], axis=0)
    determinant = coef_cc * coef_pp - coef_cp * coef_cp
    slope = (coef_pp * rhs_slope - coef_cp * rhs_inter) / determinant
    intercept = (coef_cc * rhs_inter - coef_cp * rhs_slope) / determinant
    return jnp.stack([slope, intercept])


def reference(sinogram, stat_weight, projector, block_mask, kinetic, curvature, plasma, bounds):
    integral, plasma_mean = frame_tables(bounds, plasma)
    frame_image = (integral[:, None] * kinetic[0][None, :] + plasma_mean[:, None] * kinetic[1][None, :]).astype(jnp.bfloat16)
    gates = jnp.repeat(block_mask.astype(jnp.bfloat16), NVOX // NVB, axis=1)
    matrices = projector.reshape(N_VIEW, BINS_DEV, NVOX)

    def forward(packed):
        matrix, gate_row = packed
        masked = frame_image * gate_row[None, :]
        return lax.dot_general(masked, matrix, (((1,), (1,)), ((), ())), preferred_element_type=jnp.float32)

    projection = lax.map(forward, (matrices, gates))
    projection = jnp.transpose(projection, (1, 0, 2)).reshape(FRAMES, BINS)
    residual = (stat_weight * (sinogram - projection)).astype(jnp.bfloat16)
    residual_groups = jnp.transpose(residual.reshape(FRAMES, N_VIEW, BINS_DEV), (1, 0, 2))

    def backward(running, packed):
        matrix, gate_row, rows_now = packed
        update = jnp.dot(rows_now, matrix, preferred_element_type=jnp.float32) * gate_row[None, :]
        return running + update, None

    gradient = lax.scan(backward, jnp.zeros((FRAMES, NVOX), jnp.float32), (matrices, gates, residual_groups))[0]
    frames_fine = integral[:, None] * kinetic[0][None, :] + plasma_mean[:, None] * kinetic[1][None, :]
    target = frames_fine + gradient / curvature
    rhs_slope = jnp.sum(curvature * integral[:, None] * target, axis=0)
    rhs_inter = jnp.sum(curvature * plasma_mean[:, None] * target, axis=0)
    return fit_kinetic(curvature, integral, plasma_mean, rhs_slope, rhs_inter)
```

```python
import jax
import jax.numpy as jnp
from jax import lax
from jax.experimental import pallas as pl
from jax.experimental.pallas import tpu as pltpu
from jax.sharding import PartitionSpec as P


def frame_tables(bounds, plasma):
    starts = bounds[:-1]
    finish = bounds[1:]
    seconds = jnp.arange(plasma.shape[0], dtype=jnp.int32)
    inside = ((seconds[None, :] >= starts[:, None]) & (seconds[None, :] < finish[:, None])).astype(
        jnp.float32
    )
    reaches = jnp.clip(finish[:, None] - jnp.maximum(seconds[None, :], starts[:, None]), 0).astype(
        jnp.float32
    )
    length = (finish - starts).astype(jnp.float32)
    plasma_mean = jnp.sum(inside * plasma[None, :], axis=1) / length
    integral = jnp.sum(reaches * plasma[None, :], axis=1) / (length * plasma.shape[0])
    return (integral, plasma_mean)


def split_rows(rows):
    high = lax.reduce_precision(rows, 8, 7)
    middle = lax.reduce_precision(rows - high, 8, 7)
    low = rows - high - middle
    return jnp.concatenate([high, middle, low], axis=0).astype(jnp.bfloat16)


def solve(curvature, integral, plasma_mean, kinetic, slope_sum, inter_sum):
    coef_cc = jnp.sum(curvature * (integral * integral)[:, None], axis=0)
    coef_cp = jnp.sum(curvature * (integral * plasma_mean)[:, None], axis=0)
    coef_pp = jnp.sum(curvature * (plasma_mean * plasma_mean)[:, None], axis=0)
    determinant = coef_cc * coef_pp - coef_cp * coef_cp
    slope = kinetic[0] + (coef_pp * slope_sum - coef_cp * inter_sum) / determinant
    intercept = kinetic[1] + (coef_cc * inter_sum - coef_cp * slope_sum) / determinant
    return jnp.stack([slope, intercept])


def plain(sinogram, stat_weight, projector, block_mask, kinetic, curvature, plasma, bounds):
    integral, plasma_mean = frame_tables(bounds, plasma)
    frame_rows = sinogram.shape[0]
    first_row = lax.axis_index("frame") * frame_rows
    own_integral = lax.dynamic_slice_in_dim(integral, first_row, frame_rows, 0)
    own_level = lax.dynamic_slice_in_dim(plasma_mean, first_row, frame_rows, 0)
    voxels = projector.shape[1]
    gates = jnp.repeat(block_mask[0].astype(jnp.bfloat16), voxels // block_mask.shape[1])
    portion = lax.all_gather(kinetic, ("view", "frame"), axis=1, tiled=True)
    images = (
        own_integral[:, None] * portion[0][None, :] + own_level[:, None] * portion[1][None, :]
    ).astype(jnp.bfloat16)
    images = images * gates
    projection = lax.dot_general(
        images, projector, (((1,), (1,)), ((), ())), preferred_element_type=jnp.float32
    )
    residual = lax.reduce_precision(stat_weight * (sinogram - projection), 8, 7)
    weighted = jnp.stack(
        [
            jnp.sum(own_integral[:, None] * residual, axis=0),
            jnp.sum(own_level[:, None] * residual, axis=0),
        ]
    )
    parts = jnp.dot(split_rows(weighted), projector, preferred_element_type=jnp.float32)
    partial = (parts[0:2] + parts[2:4] + parts[4:6]) * gates[None, :]
    owned = lax.psum_scatter(partial, ("view", "frame"), scatter_dimension=1, tiled=True)
    return solve(curvature, integral, plasma_mean, kinetic, owned[0], owned[1])


MESH = pl.DeviceIdType.MESH
PIECES = 6


def rounded(values):
    return values.astype(jnp.bfloat16).astype(jnp.float32)


def kernel(
    kinetic_ref, plasma_ref, sinogram_ref, weight_ref, bounds_ref, mask_ref, projector_ref, curvature_ref,
    out_ref,
    kin, mat, curv, coef, counts, proj, xsend, xrecv, zsend, zrecv, lhs,
    mat_sem, curv_sem, ksend_x, ksend_z, ksend_own, krecv, count_sem, proj_sem, xs_sem, xr_sem, zs_sem, zr_sem,
):
    view = lax.axis_index("view")
    core = lax.axis_index("frame")
    z, x = view // 2, view % 2
    inner = (z % 2 + z // 2) % 2
    shard = kinetic_ref.shape[1]
    wide = kin.shape[2]
    piece = wide // PIECES
    pad = wide - shard
    frames = curvature_ref.shape[0]
    bins = projector_ref.shape[0]
    samples = plasma_ref.shape[1]
    blocks = mask_ref.shape[1] // 16
    block = shard // blocks
    near = [z, z + 1 - 2 * (z % 2), 2 - z // 2, 3 - 3 * (z // 2)]

    def there(z_to, x_to):
        return {"view": z_to * 2 + x_to}

    other = {"frame": 1 - core}

    def mat_copy(slot):
        start = pl.multiple_of(slot * (2 * shard) + core * (2 * shard - wide), 128)
        return pltpu.make_async_copy(
            projector_ref.at[:, pl.ds(start, wide)], mat.at[slot], mat_sem.at[slot]
        )

    barrier = pltpu.get_barrier_semaphore()
    pl.semaphore_signal(barrier, inc=1, device_id=there(z, 1 - x), device_id_type=MESH)
    pl.semaphore_signal(barrier, inc=1, device_id=other, device_id_type=MESH)

    @pl.when(z > 0)
    def _():
        pl.semaphore_signal(barrier, inc=1, device_id=there(z - 1, x), device_id_type=MESH)

    @pl.when(z < 3)
    def _():
        pl.semaphore_signal(barrier, inc=1, device_id=there(z + 1, x), device_id_type=MESH)

    blank = jnp.zeros((2, pad), jnp.float32)

    @pl.when(core == 0)
    def _():
        kin[view] = jnp.concatenate([kinetic_ref[...], blank], axis=1)

    @pl.when(core == 1)
    def _():
        kin[view] = jnp.concatenate([blank, kinetic_ref[...]], axis=1)

    counts[core, 0] = sinogram_ref[...]
    counts[core, 1] = weight_ref[...]
    pl.semaphore_wait(barrier, 3 + inner)

    def send_kin(slot, sem, device):
        return pltpu.make_async_remote_copy(
            src_ref=kin.at[slot], dst_ref=kin.at[slot], send_sem=sem, recv_sem=krecv.at[slot],
            device_id=device, device_id_type=MESH,
        )

    @pl.when(z > 0)
    def _():
        send_kin(view, ksend_own.at[0], there(z - 1, x)).start()

    @pl.when(z < 3)
    def _():
        send_kin(view, ksend_own.at[1], there(z + 1, x)).start()

    send_kin(view, ksend_x.at[0], there(z, 1 - x)).start()
    count_copy = pltpu.make_async_remote_copy(
        src_ref=counts.at[core], dst_ref=counts.at[core], send_sem=count_sem.at[0], recv_sem=count_sem.at[1],
        device_id=other, device_id_type=MESH,
    )
    count_copy.start()
    for k in range(4):
        for side in (x, 1 - x):
            mat_copy(near[k] * 2 + side).start()
    curv_copy = pltpu.make_async_copy(curvature_ref, curv, curv_sem)
    curv_copy.start()

    rows = lax.broadcasted_iota(jnp.int32, (frames, 1), 0)
    starts = jnp.zeros((frames, 1), jnp.int32)
    finish = jnp.zeros((frames, 1), jnp.int32)
    for f in range(frames):
        starts = jnp.where(rows == f, bounds_ref[f], starts)
        finish = jnp.where(rows == f, bounds_ref[f + 1], finish)
    seconds = lax.broadcasted_iota(jnp.int32, (frames, samples), 1)
    plasma = plasma_ref[...]
    inside = jnp.where((seconds >= starts) & (seconds < finish), plasma, 0.0)
    reaches = jnp.maximum(finish - jnp.maximum(seconds, starts), 0).astype(jnp.float32) * plasma
    length = (finish - starts).astype(jnp.float32)
    level = jnp.sum(inside, axis=1, keepdims=True) / length
    integral = jnp.sum(reaches, axis=1, keepdims=True) / (length * samples)

    def gate_row(slot, sub):
        first = (slot * 2 + core) * blocks
        lane = lax.broadcasted_iota(jnp.int32, (1, piece), 1) + (sub * piece - core * pad)
        row = jnp.full((1, piece), mask_ref[0, first], jnp.int32)
        for i in range(1, blocks):
            row = jnp.where(lane >= i * block, mask_ref[0, first + i], row)
        return row.astype(jnp.float32)

    def forward(slot, total):
        mat_copy(slot).wait()

        def step(sub, total):
            cols = pl.ds(pl.multiple_of(sub * piece, 128), piece)
            gates = gate_row(slot, sub)
            slope = kin[slot, 0:1, cols] * gates
            inter = kin[slot, 1:2, cols] * gates
            images = (integral * slope + level * inter).astype(jnp.bfloat16)
            return total + lax.dot_general(
                images, mat[slot, :, cols], (((1,), (1,)), ((), ())), preferred_element_type=jnp.float32
            )

        return lax.fori_loop(0, PIECES, step, total)

    total = jnp.zeros((frames, bins), jnp.float32)
    for k in range(4):
        slot = near[k] * 2 + x
        if k > 0:
            onward = 3 - z if k == 1 else 3 * (z // 2)
            send_kin(slot, ksend_x.at[k], there(z, 1 - x)).wait_recv()

            @pl.when(inner == 1)
            def _():
                send_kin(slot, ksend_z.at[k - 1], there(onward, x)).start()

            send_kin(slot, ksend_x.at[k], there(z, 1 - x)).start()
        total = forward(slot, total)
        if k == 0:
            curv_copy.wait()
            for start in range(0, shard, piece):
                size = min(piece, shard - start)
                c = curv[:, start:start + size]
                cc = jnp.sum(c * (integral * integral), axis=0, keepdims=True)
                cp = jnp.sum(c * (integral * level), axis=0, keepdims=True)
                pp = jnp.sum(c * (level * level), axis=0, keepdims=True)
                scale = 1.0 / (cc * pp - cp * cp)
                coef[0:1, start:start + size] = cc * scale
                coef[1:2, start:start + size] = cp * scale
                coef[2:3, start:start + size] = pp * scale
        if k > 0:
            past = near[k - 1] * 2 + (1 - x)
            send_kin(past, ksend_x.at[0], there(z, 1 - x)).wait_recv()
            total = forward(past, total)
    past = near[3] * 2 + (1 - x)
    send_kin(past, ksend_x.at[0], there(z, 1 - x)).wait_recv()
    total = forward(past, total)

    proj[core] = total
    proj_copy = pltpu.make_async_remote_copy(
        src_ref=proj.at[core], dst_ref=proj.at[core], send_sem=proj_sem.at[0], recv_sem=proj_sem.at[1],
        device_id=other, device_id_type=MESH,
    )
    proj_copy.start()
    count_copy.wait()
    proj_copy.wait()
    projection = proj[0] + proj[1]
    sinogram = jnp.concatenate([counts[0, 0], counts[1, 0]], axis=0)
    weight = jnp.concatenate([counts[0, 1], counts[1, 1]], axis=0)
    residual = rounded(weight * (sinogram - projection))
    slope_row = jnp.sum(integral * residual, axis=0, keepdims=True)
    inter_row = jnp.sum(level * residual, axis=0, keepdims=True)
    index = lax.broadcasted_iota(jnp.int32, (16, bins), 0)
    both = jnp.where(index % 2 == 0, slope_row, inter_row)
    high = rounded(both)
    middle = rounded(both - high)
    low = both - high - middle
    lhs[...] = jnp.where(
        index < 2, high, jnp.where(index < 4, middle, jnp.where(index < 6, low, 0.0))
    ).astype(jnp.bfloat16)

    def back(slot, sub):
        cols = pl.ds(pl.multiple_of(sub * piece, 128), piece)
        parts = jnp.dot(lhs[...], mat[slot, :, cols], preferred_element_type=jnp.float32)
        return (parts[0:2] + parts[2:4] + parts[4:6]) * gate_row(slot, sub), cols

    owners = near[::-1]

    def xcopy(k):
        return pltpu.make_async_remote_copy(
            src_ref=xsend.at[k], dst_ref=xrecv.at[k], send_sem=xs_sem.at[k], recv_sem=xr_sem.at[k],
            device_id=there(z, 1 - x), device_id_type=MESH,
        )

    def zcopy(k):
        if k == 2:
            to, place = near[1], 4 + z % 2
        else:
            to = z + 1 - 2 * (z // 2)
            place = owners[0] if k == 0 else (1 - inner) * owners[1] + inner * (4 + z // 2)
        return pltpu.make_async_remote_copy(
            src_ref=zsend.at[k], dst_ref=zrecv.at[place], send_sem=zs_sem.at[k], recv_sem=zr_sem.at[place],
            device_id=there(to, x), device_id_type=MESH,
        )

    def arrived(place):
        pltpu.make_async_remote_copy(
            src_ref=zrecv.at[place], dst_ref=zrecv.at[place], send_sem=zs_sem.at[0], recv_sem=zr_sem.at[place],
            device_id=there(z, 1 - x), device_id_type=MESH,
        ).wait_recv()

    for k in range(4):

        @pl.loop(0, PIECES)
        def _(sub):
            values, cols = back(owners[k] * 2 + 1 - x, sub)
            xsend[k, :, cols] = values

        xcopy(k).start()
    for k in range(4):

        @pl.loop(0, PIECES)
        def _(sub):
            values, cols = back(owners[k] * 2 + x, sub)
            zsend[k, :, cols] = values

    for k in range(4):
        xcopy(k).wait_recv()
        if k < 3:

            @pl.when(inner == 1)
            def _():
                arrived(owners[k])
                zsend[k] = zsend[k] + xrecv[k] + zrecv[owners[k]]

            @pl.when(inner == 0)
            def _():
                zsend[k] = zsend[k] + xrecv[k]

            zcopy(k).start()

    @pl.when(inner == 1)
    def _():
        arrived(4)
        arrived(5)
        zsend[3] = zsend[3] + xrecv[3] + zrecv[4] + zrecv[5]

    @pl.when(inner == 0)
    def _():
        arrived(5 - z // 2)
        zsend[3] = zsend[3] + xrecv[3] + zrecv[5 - z // 2]

    def finish_with(shift):
        slope = zsend[3, 0:1, shift:shift + shard]
        inter = zsend[3, 1:2, shift:shift + shard]
        cc, cp, pp = coef[0:1], coef[1:2], coef[2:3]
        out_ref[0:1] = kinetic_ref[0:1] + (pp * slope - cp * inter)
        out_ref[1:2] = kinetic_ref[1:2] + (cc * inter - cp * slope)

    @pl.when(core == 0)
    def _():
        finish_with(0)

    @pl.when(core == 1)
    def _():
        finish_with(pad)

    for k in range(4):
        xcopy(k).wait_send()
        send_kin(near[k] * 2 + x, ksend_x.at[k], there(z, 1 - x)).wait_send()
    for k in range(3):
        zcopy(k).wait_send()

    @pl.when(inner == 1)
    def _():
        for k in range(1, 4):
            send_kin(near[k] * 2 + x, ksend_z.at[k - 1], there(z, 1 - x)).wait_send()

    @pl.when(z > 0)
    def _():
        send_kin(view, ksend_own.at[0], there(z - 1, x)).wait_send()

    @pl.when(z < 3)
    def _():
        send_kin(view, ksend_own.at[1], there(z + 1, x)).wait_send()


def fused(sinogram, stat_weight, projector, block_mask, kinetic, curvature, plasma, bounds):
    shard = kinetic.shape[1]
    frames = curvature.shape[0]
    bins = projector.shape[0]
    wide = padded_width(shard)
    dma = pltpu.SemaphoreType.DMA
    vmem = pl.BlockSpec(memory_space=pltpu.VMEM)
    smem = pl.BlockSpec(memory_space=pltpu.SMEM)
    hbm = pl.BlockSpec(memory_space=pl.ANY)
    f32 = jnp.float32
    return pl.pallas_call(
        kernel,
        out_shape=jax.ShapeDtypeStruct(kinetic.shape, f32),
        in_specs=[vmem, vmem, vmem, vmem, smem, smem, hbm, hbm],
        out_specs=vmem,
        scratch_shapes=[
            pltpu.VMEM((8, 2, wide), f32),
            pltpu.VMEM((8, bins, wide), jnp.bfloat16),
            pltpu.VMEM((frames, shard), f32),
            pltpu.VMEM((3, shard), f32),
            pltpu.VMEM((2, 2) + sinogram.shape, f32),
            pltpu.VMEM((2, frames, bins), f32),
            pltpu.VMEM((4, 2, wide), f32),
            pltpu.VMEM((4, 2, wide), f32),
            pltpu.VMEM((4, 2, wide), f32),
            pltpu.VMEM((6, 2, wide), f32),
            pltpu.VMEM((16, bins), jnp.bfloat16),
            dma((8,)),
            dma,
            dma((4,)),
            dma((3,)),
            dma((2,)),
            dma((8,)),
            dma((2,)),
            dma((2,)),
            dma((4,)),
            dma((4,)),
            dma((3,)),
            dma((6,)),
        ],
        compiler_params=pltpu.CompilerParams(
            collective_id=0, has_side_effects=True, vmem_limit_bytes=40 * 2**20
        ),
        cost_estimate=pl.CostEstimate(
            flops=2 * frames * projector.size, bytes_accessed=projector.size, transcendentals=0
        ),
    )(kinetic, plasma[None, :], sinogram, stat_weight, bounds, block_mask, projector, curvature)


def padded_width(shard):
    step = 128 * PIECES
    return -(-shard // step) * step


def fits(mesh, projector, block_mask, kinetic, sinogram):
    shard = kinetic.shape[1]
    return (
        mesh.shape["view"] == 8
        and mesh.shape["frame"] == 2
        and 2 * shard % 128 == 0
        and padded_width(shard) <= 2 * shard
        and block_mask.shape[1] % 16 == 0
        and projector.shape == (16, 16 * shard)
        and sinogram.shape == (8, 16)
    )


def solution(mesh):
    in_specs = (
        P(("grp", "frame"), "view"),
        P(("grp", "frame"), "view"),
        P("view", None),
        P("view", None),
        P(None, ("grp", "view", "frame")),
        P(None, ("grp", "view", "frame")),
        P("grp"),
        P("grp"),
    )
    out_specs = P(None, ("grp", "view", "frame"))

    def local(sinogram, stat_weight, projector, block_mask, kinetic, curvature, plasma, bounds):
        form = fused if fits(mesh, projector, block_mask, kinetic, sinogram) else plain
        return form(sinogram, stat_weight, projector, block_mask, kinetic, curvature, plasma, bounds)

    return jax.shard_map(local, mesh=mesh, in_specs=in_specs, out_specs=out_specs, check_vma=False)
```

```python
import jax
import jax.numpy as jnp
from jax import lax
from jax.experimental import pallas as pl
from jax.experimental.pallas import tpu as pltpu
from jax.sharding import PartitionSpec as P


def frame_tables(bounds, plasma):
    starts = bounds[:-1]
    finish = bounds[1:]
    seconds = jnp.arange(plasma.shape[0], dtype=jnp.int32)
    inside = ((seconds[None, :] >= starts[:, None]) & (seconds[None, :] < finish[:, None])).astype(
        jnp.float32
    )
    reaches = jnp.clip(finish[:, None] - jnp.maximum(seconds[None, :], starts[:, None]), 0).astype(
        jnp.float32
    )
    length = (finish - starts).astype(jnp.float32)
    plasma_mean = jnp.sum(inside * plasma[None, :], axis=1) / length
    integral = jnp.sum(reaches * plasma[None, :], axis=1) / (length * plasma.shape[0])
    return (integral, plasma_mean)


def split_rows(rows):
    high = lax.reduce_precision(rows, 8, 7)
    middle = lax.reduce_precision(rows - high, 8, 7)
    low = rows - high - middle
    return jnp.concatenate([high, middle, low], axis=0).astype(jnp.bfloat16)


def solve(curvature, integral, plasma_mean, kinetic, slope_sum, inter_sum):
    coef_cc = jnp.sum(curvature * (integral * integral)[:, None], axis=0)
    coef_cp = jnp.sum(curvature * (integral * plasma_mean)[:, None], axis=0)
    coef_pp = jnp.sum(curvature * (plasma_mean * plasma_mean)[:, None], axis=0)
    determinant = coef_cc * coef_pp - coef_cp * coef_cp
    slope = kinetic[0] + (coef_pp * slope_sum - coef_cp * inter_sum) / determinant
    intercept = kinetic[1] + (coef_cc * inter_sum - coef_cp * slope_sum) / determinant
    return jnp.stack([slope, intercept])


def plain(sinogram, stat_weight, projector, block_mask, kinetic, curvature, plasma, bounds):
    integral, plasma_mean = frame_tables(bounds, plasma)
    frame_rows = sinogram.shape[0]
    first_row = lax.axis_index("frame") * frame_rows
    own_integral = lax.dynamic_slice_in_dim(integral, first_row, frame_rows, 0)
    own_level = lax.dynamic_slice_in_dim(plasma_mean, first_row, frame_rows, 0)
    voxels = projector.shape[1]
    gates = jnp.repeat(block_mask[0].astype(jnp.bfloat16), voxels // block_mask.shape[1])
    portion = lax.all_gather(kinetic, ("view", "frame"), axis=1, tiled=True)
    images = (
        own_integral[:, None] * portion[0][None, :] + own_level[:, None] * portion[1][None, :]
    ).astype(jnp.bfloat16)
    images = images * gates
    projection = lax.dot_general(
        images, projector, (((1,), (1,)), ((), ())), preferred_element_type=jnp.float32
    )
    residual = lax.reduce_precision(stat_weight * (sinogram - projection), 8, 7)
    weighted = jnp.stack(
        [
            jnp.sum(own_integral[:, None] * residual, axis=0),
            jnp.sum(own_level[:, None] * residual, axis=0),
        ]
    )
    parts = jnp.dot(split_rows(weighted), projector, preferred_element_type=jnp.float32)
    partial = (parts[0:2] + parts[2:4] + parts[4:6]) * gates[None, :]
    owned = lax.psum_scatter(partial, ("view", "frame"), scatter_dimension=1, tiled=True)
    return solve(curvature, integral, plasma_mean, kinetic, owned[0], owned[1])


MESH = pl.DeviceIdType.MESH
PIECES = 6
PARTS = 6


def rounded(values):
    return values.astype(jnp.bfloat16).astype(jnp.float32)


def kernel(
    kinetic_hbm, plasma_hbm, sinogram_hbm, weight_hbm, bounds_hbm, mask_hbm, projector_ref, curvature_ref,
    out_ref,
    kinetic_ref, plasma_ref, bounds_ref, mask_ref, in_sem,
    kin, mat, curv, coef, counts, proj, xsend, xrecv, zsend, zrecv, lhs,
    mat_sem, curv_sem, ksend_x, ksend_z, ksend_own, krecv, count_sem, proj_sem, xs_sem, xr_sem, zs_sem, zr_sem,
):
    view = lax.axis_index("view")
    core = lax.axis_index("frame")
    z, x = view // 2, view % 2
    inner = (z % 2 + z // 2) % 2
    shard = kinetic_ref.shape[1]
    wide = kin.shape[2]
    piece = wide // PIECES
    span = wide // PARTS
    each = PIECES // PARTS
    pad = wide - shard
    frames = curvature_ref.shape[0]
    bins = projector_ref.shape[0]
    samples = plasma_ref.shape[1]
    blocks = mask_ref.shape[1] // 16
    block = shard // blocks
    near = [z, z + 1 - 2 * (z % 2), 2 - z // 2, 3 - 3 * (z // 2)]

    def there(z_to, x_to):
        return {"view": z_to * 2 + x_to}

    other = {"frame": 1 - core}

    def mat_copy(slot):
        start = pl.multiple_of(slot * (2 * shard) + core * (2 * shard - wide), 128)
        return pltpu.make_async_copy(
            projector_ref.at[:, pl.ds(start, wide)], mat.at[slot], mat_sem.at[slot]
        )

    inputs = [
        pltpu.make_async_copy(source, place, in_sem.at[i])
        for i, (source, place) in enumerate(
            [
                (kinetic_hbm, kinetic_ref),
                (plasma_hbm, plasma_ref.at[0]),
                (sinogram_hbm, counts.at[core, 0]),
                (weight_hbm, counts.at[core, 1]),
                (bounds_hbm, bounds_ref),
                (mask_hbm, mask_ref),
            ]
        )
    ]
    for copy in inputs:
        copy.start()
    barrier = pltpu.get_barrier_semaphore()
    pl.semaphore_signal(barrier, inc=1, device_id=there(z, 1 - x), device_id_type=MESH)
    pl.semaphore_signal(barrier, inc=1, device_id=other, device_id_type=MESH)

    @pl.when(z > 0)
    def _():
        pl.semaphore_signal(barrier, inc=1, device_id=there(z - 1, x), device_id_type=MESH)

    @pl.when(z < 3)
    def _():
        pl.semaphore_signal(barrier, inc=1, device_id=there(z + 1, x), device_id_type=MESH)

    inputs[0].wait()
    blank = jnp.zeros((2, pad), jnp.float32)

    @pl.when(core == 0)
    def _():
        kin[view] = jnp.concatenate([kinetic_ref[...], blank], axis=1)

    @pl.when(core == 1)
    def _():
        kin[view] = jnp.concatenate([blank, kinetic_ref[...]], axis=1)

    pl.semaphore_wait(barrier, 3 + inner)

    def part(q):
        return pl.ds(pl.multiple_of(q * span, 128), span)

    def send_kin(slot, q, sem, device):
        return pltpu.make_async_remote_copy(
            src_ref=kin.at[slot, :, part(q)], dst_ref=kin.at[slot, :, part(q)],
            send_sem=sem, recv_sem=krecv.at[slot, q], device_id=device, device_id_type=MESH,
        )

    across = there(z, 1 - x)

    @pl.loop(0, PARTS)
    def _(q):
        @pl.when(z > 0)
        def _():
            send_kin(view, q, ksend_own.at[0, q], there(z - 1, x)).start()

        @pl.when(z < 3)
        def _():
            send_kin(view, q, ksend_own.at[1, q], there(z + 1, x)).start()

        send_kin(view, q, ksend_x.at[0, q], across).start()

    count_copy = pltpu.make_async_remote_copy(
        src_ref=counts.at[core], dst_ref=counts.at[core], send_sem=count_sem.at[0], recv_sem=count_sem.at[1],
        device_id=other, device_id_type=MESH,
    )
    inputs[2].wait()
    inputs[3].wait()
    count_copy.start()
    for k in range(4):
        for side in (x, 1 - x):
            mat_copy(near[k] * 2 + side).start()
    curv_copy = pltpu.make_async_copy(curvature_ref, curv, curv_sem)
    curv_copy.start()

    for i in (1, 4, 5):
        inputs[i].wait()
    rows = lax.broadcasted_iota(jnp.int32, (frames, 1), 0)
    starts = jnp.zeros((frames, 1), jnp.int32)
    finish = jnp.zeros((frames, 1), jnp.int32)
    for f in range(frames):
        starts = jnp.where(rows == f, bounds_ref[f], starts)
        finish = jnp.where(rows == f, bounds_ref[f + 1], finish)
    seconds = lax.broadcasted_iota(jnp.int32, (frames, samples), 1)
    plasma = plasma_ref[...]
    inside = jnp.where((seconds >= starts) & (seconds < finish), plasma, 0.0)
    reaches = jnp.maximum(finish - jnp.maximum(seconds, starts), 0).astype(jnp.float32) * plasma
    length = (finish - starts).astype(jnp.float32)
    level = jnp.sum(inside, axis=1, keepdims=True) / length
    integral = jnp.sum(reaches, axis=1, keepdims=True) / (length * samples)

    def gate_row(slot, sub):
        first = (slot * 2 + core) * blocks
        lane = lax.broadcasted_iota(jnp.int32, (1, piece), 1) + (sub * piece - core * pad)
        row = jnp.full((1, piece), mask_ref[0, first], jnp.int32)
        for i in range(1, blocks):
            row = jnp.where(lane >= i * block, mask_ref[0, first + i], row)
        return row.astype(jnp.float32)

    def forward(slot, total, landed):
        mat_copy(slot).wait()

        def step(sub, total):
            cols = pl.ds(pl.multiple_of(sub * piece, 128), piece)
            gates = gate_row(slot, sub)
            slope = kin[slot, 0:1, cols] * gates
            inter = kin[slot, 1:2, cols] * gates
            images = (integral * slope + level * inter).astype(jnp.bfloat16)
            return total + lax.dot_general(
                images, mat[slot, :, cols], (((1,), (1,)), ((), ())), preferred_element_type=jnp.float32
            )

        for q in range(PARTS):
            if not landed:
                send_kin(slot, q, ksend_x.at[0, q], across).wait_recv()
            total = lax.fori_loop(q * each, (q + 1) * each, step, total)
        return total

    total = jnp.zeros((frames, bins), jnp.float32)
    total = forward(view, total, True)
    curv_copy.wait()
    for start in range(0, shard, piece):
        size = min(piece, shard - start)
        c = curv[:, start:start + size]
        cc = jnp.sum(c * (integral * integral), axis=0, keepdims=True)
        cp = jnp.sum(c * (integral * level), axis=0, keepdims=True)
        pp = jnp.sum(c * (level * level), axis=0, keepdims=True)
        scale = 1.0 / (cc * pp - cp * cp)
        coef[0:1, start:start + size] = cc * scale
        coef[1:2, start:start + size] = cp * scale
        coef[2:3, start:start + size] = pp * scale

    def relay(k, q, onward):
        slot = near[k] * 2 + x
        send_kin(slot, q, ksend_x.at[k, q], across).wait_recv()
        if onward is not None:
            send_kin(slot, q, ksend_z.at[k - 1, q], there(onward, x)).start()
        send_kin(slot, q, ksend_x.at[k, q], across).start()

    @pl.when(inner == 0)
    def _():
        for k in range(1, 4):

            @pl.loop(0, PARTS)
            def _(q):
                relay(k, q, None)

    @pl.when(inner == 1)
    def _():
        @pl.loop(0, PARTS)
        def _(q):
            relay(1, q, 3 - z)
            relay(2, q, 3 * (z // 2))

        @pl.loop(0, PARTS)
        def _(q):
            relay(3, q, 3 * (z // 2))

    for k in range(1, 4):
        total = forward(near[k] * 2 + x, total, True)
    for k in range(4):
        total = forward(near[k] * 2 + (1 - x), total, False)

    proj[core] = total
    proj_copy = pltpu.make_async_remote_copy(
        src_ref=proj.at[core], dst_ref=proj.at[core], send_sem=proj_sem.at[0], recv_sem=proj_sem.at[1],
        device_id=other, device_id_type=MESH,
    )
    proj_copy.start()
    count_copy.wait()
    proj_copy.wait()
    projection = proj[0] + proj[1]
    sinogram = jnp.concatenate([counts[0, 0], counts[1, 0]], axis=0)
    weight = jnp.concatenate([counts[0, 1], counts[1, 1]], axis=0)
    residual = rounded(weight * (sinogram - projection))
    slope_row = jnp.sum(integral * residual, axis=0, keepdims=True)
    inter_row = jnp.sum(level * residual, axis=0, keepdims=True)
    index = lax.broadcasted_iota(jnp.int32, (16, bins), 0)
    both = jnp.where(index % 2 == 0, slope_row, inter_row)
    high = rounded(both)
    middle = rounded(both - high)
    low = both - high - middle
    lhs[...] = jnp.where(
        index < 2, high, jnp.where(index < 4, middle, jnp.where(index < 6, low, 0.0))
    ).astype(jnp.bfloat16)

    def back(slot, sub):
        cols = pl.ds(pl.multiple_of(sub * piece, 128), piece)
        parts = jnp.dot(lhs[...], mat[slot, :, cols], preferred_element_type=jnp.float32)
        return (parts[0:2] + parts[2:4] + parts[4:6]) * gate_row(slot, sub), cols

    owners = near[::-1]

    def xcopy(k, q):
        return pltpu.make_async_remote_copy(
            src_ref=xsend.at[k, :, part(q)], dst_ref=xrecv.at[k, :, part(q)],
            send_sem=xs_sem.at[k, q], recv_sem=xr_sem.at[k, q], device_id=across, device_id_type=MESH,
        )

    def zcopy(k, q):
        if k == 2:
            to, place = near[1], 4 + z % 2
        else:
            to = z + 1 - 2 * (z // 2)
            place = owners[0] if k == 0 else (1 - inner) * owners[1] + inner * (4 + z // 2)
        return pltpu.make_async_remote_copy(
            src_ref=zsend.at[k, :, part(q)], dst_ref=zrecv.at[place, :, part(q)],
            send_sem=zs_sem.at[k, q], recv_sem=zr_sem.at[place, q],
            device_id=there(to, x), device_id_type=MESH,
        )

    def arrived(place, q):
        pltpu.make_async_remote_copy(
            src_ref=zrecv.at[place, :, part(q)], dst_ref=zrecv.at[place, :, part(q)],
            send_sem=zs_sem.at[0, q], recv_sem=zr_sem.at[place, q], device_id=across, device_id_type=MESH,
        ).wait_recv()

    for k in range(4):

        @pl.loop(0, PARTS)
        def _(q):
            for i in range(each):
                values, cols = back(owners[k] * 2 + 1 - x, q * each + i)
                xsend[k, :, cols] = values
            xcopy(k, q).start()

    for k in range(4):

        @pl.loop(0, PARTS)
        def _(q):
            for i in range(each):
                values, cols = back(owners[k] * 2 + x, q * each + i)
                zsend[k, :, cols] = values
            cols = part(q)
            xcopy(k, q).wait_recv()

            @pl.when(inner == 1)
            def _():
                places = (owners[k],) if k < 3 else (4, 5)
                rest = xrecv[k, :, cols]
                for place in places:
                    arrived(place, q)
                    rest = rest + zrecv[place, :, cols]
                zsend[k, :, cols] = zsend[k, :, cols] + rest

            @pl.when(inner == 0)
            def _():
                rest = xrecv[k, :, cols]
                if k == 3:
                    arrived(5 - z // 2, q)
                    rest = rest + zrecv[5 - z // 2, :, cols]
                zsend[k, :, cols] = zsend[k, :, cols] + rest

            if k < 3:
                zcopy(k, q).start()

    def finish_with(shift):
        slope = zsend[3, 0:1, shift:shift + shard]
        inter = zsend[3, 1:2, shift:shift + shard]
        cc, cp, pp = coef[0:1], coef[1:2], coef[2:3]
        out_ref[0:1] = kinetic_ref[0:1] + (pp * slope - cp * inter)
        out_ref[1:2] = kinetic_ref[1:2] + (cc * inter - cp * slope)

    @pl.when(core == 0)
    def _():
        finish_with(0)

    @pl.when(core == 1)
    def _():
        finish_with(pad)

    @pl.loop(0, PARTS)
    def _(q):
        for k in range(4):
            xcopy(k, q).wait_send()
            send_kin(near[k] * 2 + x, q, ksend_x.at[k, q], across).wait_send()
        for k in range(3):
            zcopy(k, q).wait_send()

        @pl.when(inner == 1)
        def _():
            for k in range(1, 4):
                send_kin(near[k] * 2 + x, q, ksend_z.at[k - 1, q], across).wait_send()

        @pl.when(z > 0)
        def _():
            send_kin(view, q, ksend_own.at[0, q], across).wait_send()

        @pl.when(z < 3)
        def _():
            send_kin(view, q, ksend_own.at[1, q], across).wait_send()


def fused(sinogram, stat_weight, projector, block_mask, kinetic, curvature, plasma, bounds):
    shard = kinetic.shape[1]
    frames = curvature.shape[0]
    bins = projector.shape[0]
    wide = padded_width(shard)
    dma = pltpu.SemaphoreType.DMA
    vmem = pl.BlockSpec(memory_space=pltpu.VMEM)
    hbm = pl.BlockSpec(memory_space=pl.ANY)
    f32 = jnp.float32
    return pl.pallas_call(
        kernel,
        out_shape=jax.ShapeDtypeStruct(kinetic.shape, f32),
        in_specs=[hbm] * 8,
        out_specs=vmem,
        scratch_shapes=[
            pltpu.VMEM(kinetic.shape, f32),
            pltpu.VMEM((1,) + plasma.shape, f32),
            pltpu.SMEM(bounds.shape, jnp.int32),
            pltpu.SMEM(block_mask.shape, jnp.int32),
            dma((6,)),
            pltpu.VMEM((8, 2, wide), f32),
            pltpu.VMEM((8, bins, wide), jnp.bfloat16),
            pltpu.VMEM((frames, shard), f32),
            pltpu.VMEM((3, shard), f32),
            pltpu.VMEM((2, 2) + sinogram.shape, f32),
            pltpu.VMEM((2, frames, bins), f32),
            pltpu.VMEM((4, 2, wide), f32),
            pltpu.VMEM((4, 2, wide), f32),
            pltpu.VMEM((4, 2, wide), f32),
            pltpu.VMEM((6, 2, wide), f32),
            pltpu.VMEM((16, bins), jnp.bfloat16),
            dma((8,)),
            dma,
            dma((4, PARTS)),
            dma((3, PARTS)),
            dma((2, PARTS)),
            dma((8, PARTS)),
            dma((2,)),
            dma((2,)),
            dma((4, PARTS)),
            dma((4, PARTS)),
            dma((3, PARTS)),
            dma((6, PARTS)),
        ],
        compiler_params=pltpu.CompilerParams(
            collective_id=0, has_side_effects=True, vmem_limit_bytes=56 * 2**20
        ),
        cost_estimate=pl.CostEstimate(
            flops=2 * frames * projector.size, bytes_accessed=projector.size, transcendentals=0
        ),
    )(kinetic, plasma, sinogram, stat_weight, bounds, block_mask, projector, curvature)


def padded_width(shard):
    step = 128 * PIECES
    return -(-shard // step) * step


def fits(mesh, projector, block_mask, kinetic, sinogram):
    shard = kinetic.shape[1]
    return (
        mesh.shape["view"] == 8
        and mesh.shape["frame"] == 2
        and 2 * shard % 128 == 0
        and padded_width(shard) <= 2 * shard
        and block_mask.shape[1] % 16 == 0
        and projector.shape == (16, 16 * shard)
        and sinogram.shape == (8, 16)
    )


def solution(mesh):
    in_specs = (
        P(("grp", "frame"), "view"),
        P(("grp", "frame"), "view"),
        P("view", None),
        P("view", None),
        P(None, ("grp", "view", "frame")),
        P(None, ("grp", "view", "frame")),
        P("grp"),
        P("grp"),
    )
    out_specs = P(None, ("grp", "view", "frame"))

    def local(sinogram, stat_weight, projector, block_mask, kinetic, curvature, plasma, bounds):
        form = fused if fits(mesh, projector, block_mask, kinetic, sinogram) else plain
        return form(sinogram, stat_weight, projector, block_mask, kinetic, curvature, plasma, bounds)

    return jax.shard_map(local, mesh=mesh, in_specs=in_specs, out_specs=out_specs, check_vma=False)
```

```python
import jax
import jax.numpy as jnp
from jax import lax
from jax.experimental import pallas as pl
from jax.experimental.pallas import tpu as pltpu
from jax.sharding import PartitionSpec as P


def frame_tables(bounds, plasma):
    starts = bounds[:-1]
    finish = bounds[1:]
    seconds = jnp.arange(plasma.shape[0], dtype=jnp.int32)
    inside = ((seconds[None, :] >= starts[:, None]) & (seconds[None, :] < finish[:, None])).astype(
        jnp.float32
    )
    reaches = jnp.clip(finish[:, None] - jnp.maximum(seconds[None, :], starts[:, None]), 0).astype(
        jnp.float32
    )
    length = (finish - starts).astype(jnp.float32)
    plasma_mean = jnp.sum(inside * plasma[None, :], axis=1) / length
    integral = jnp.sum(reaches * plasma[None, :], axis=1) / (length * plasma.shape[0])
    return (integral, plasma_mean)


def split_rows(rows):
    high = lax.reduce_precision(rows, 8, 7)
    middle = lax.reduce_precision(rows - high, 8, 7)
    low = rows - high - middle
    return jnp.concatenate([high, middle, low], axis=0).astype(jnp.bfloat16)


def solve(curvature, integral, plasma_mean, kinetic, slope_sum, inter_sum):
    coef_cc = jnp.sum(curvature * (integral * integral)[:, None], axis=0)
    coef_cp = jnp.sum(curvature * (integral * plasma_mean)[:, None], axis=0)
    coef_pp = jnp.sum(curvature * (plasma_mean * plasma_mean)[:, None], axis=0)
    determinant = coef_cc * coef_pp - coef_cp * coef_cp
    slope = kinetic[0] + (coef_pp * slope_sum - coef_cp * inter_sum) / determinant
    intercept = kinetic[1] + (coef_cc * inter_sum - coef_cp * slope_sum) / determinant
    return jnp.stack([slope, intercept])


def plain(sinogram, stat_weight, projector, block_mask, kinetic, curvature, plasma, bounds):
    integral, plasma_mean = frame_tables(bounds, plasma)
    frame_rows = sinogram.shape[0]
    first_row = lax.axis_index("frame") * frame_rows
    own_integral = lax.dynamic_slice_in_dim(integral, first_row, frame_rows, 0)
    own_level = lax.dynamic_slice_in_dim(plasma_mean, first_row, frame_rows, 0)
    voxels = projector.shape[1]
    gates = jnp.repeat(block_mask[0].astype(jnp.bfloat16), voxels // block_mask.shape[1])
    portion = lax.all_gather(kinetic, ("view", "frame"), axis=1, tiled=True)
    images = (
        own_integral[:, None] * portion[0][None, :] + own_level[:, None] * portion[1][None, :]
    ).astype(jnp.bfloat16)
    images = images * gates
    projection = lax.dot_general(
        images, projector, (((1,), (1,)), ((), ())), preferred_element_type=jnp.float32
    )
    residual = lax.reduce_precision(stat_weight * (sinogram - projection), 8, 7)
    weighted = jnp.stack(
        [
            jnp.sum(own_integral[:, None] * residual, axis=0),
            jnp.sum(own_level[:, None] * residual, axis=0),
        ]
    )
    parts = jnp.dot(split_rows(weighted), projector, preferred_element_type=jnp.float32)
    partial = (parts[0:2] + parts[2:4] + parts[4:6]) * gates[None, :]
    owned = lax.psum_scatter(partial, ("view", "frame"), scatter_dimension=1, tiled=True)
    return solve(curvature, integral, plasma_mean, kinetic, owned[0], owned[1])


MESH = pl.DeviceIdType.MESH
PIECES = 6
PARTS = 6
SUM_PARTS = 3


def rounded(values):
    return values.astype(jnp.bfloat16).astype(jnp.float32)


def kernel(
    kinetic_hbm, plasma_hbm, sinogram_hbm, weight_hbm, bounds_hbm, mask_hbm, projector_ref, curvature_ref,
    out_ref,
    kinetic_ref, plasma_ref, bounds_ref, mask_ref, in_sem,
    kin, mat, curv, coef, counts, proj, xsend, xrecv, zsend, zrecv, lhs,
    mat_sem, curv_sem, ksend_x, ksend_z, ksend_own, krecv, count_sem, proj_sem, xs_sem, xr_sem, zs_sem, zr_sem,
):
    view = lax.axis_index("view")
    core = lax.axis_index("frame")
    z, x = view // 2, view % 2
    inner = (z % 2 + z // 2) % 2
    shard = kinetic_ref.shape[1]
    wide = kin.shape[2]
    piece = wide // PIECES
    span = wide // PARTS
    each = PIECES // PARTS
    pad = wide - shard
    frames = curvature_ref.shape[0]
    bins = projector_ref.shape[0]
    samples = plasma_ref.shape[1]
    blocks = mask_ref.shape[1] // 16
    block = shard // blocks
    near = [z, z + 1 - 2 * (z % 2), 2 - z // 2, 3 - 3 * (z // 2)]

    def there(z_to, x_to):
        return {"view": z_to * 2 + x_to}

    other = {"frame": 1 - core}

    def mat_copy(slot):
        start = pl.multiple_of(slot * (2 * shard) + core * (2 * shard - wide), 128)
        return pltpu.make_async_copy(
            projector_ref.at[:, pl.ds(start, wide)], mat.at[slot], mat_sem.at[slot]
        )

    inputs = [
        pltpu.make_async_copy(source, place, in_sem.at[i])
        for i, (source, place) in enumerate(
            [
                (kinetic_hbm, kinetic_ref),
                (plasma_hbm, plasma_ref.at[0]),
                (sinogram_hbm, counts.at[core, 0]),
                (weight_hbm, counts.at[core, 1]),
                (bounds_hbm, bounds_ref),
                (mask_hbm, mask_ref),
            ]
        )
    ]
    for copy in inputs:
        copy.start()
    barrier = pltpu.get_barrier_semaphore()
    pl.semaphore_signal(barrier, inc=1, device_id=there(z, 1 - x), device_id_type=MESH)
    pl.semaphore_signal(barrier, inc=1, device_id=other, device_id_type=MESH)

    @pl.when(z > 0)
    def _():
        pl.semaphore_signal(barrier, inc=1, device_id=there(z - 1, x), device_id_type=MESH)

    @pl.when(z < 3)
    def _():
        pl.semaphore_signal(barrier, inc=1, device_id=there(z + 1, x), device_id_type=MESH)

    inputs[0].wait()
    blank = jnp.zeros((2, pad), jnp.float32)

    @pl.when(core == 0)
    def _():
        kin[view] = jnp.concatenate([kinetic_ref[...], blank], axis=1)

    @pl.when(core == 1)
    def _():
        kin[view] = jnp.concatenate([blank, kinetic_ref[...]], axis=1)

    pl.semaphore_wait(barrier, 3 + inner)

    def part(q):
        return pl.ds(pl.multiple_of(q * span, 128), span)

    def send_kin(slot, q, sem, device):
        return pltpu.make_async_remote_copy(
            src_ref=kin.at[slot, :, part(q)], dst_ref=kin.at[slot, :, part(q)],
            send_sem=sem, recv_sem=krecv.at[slot, q], device_id=device, device_id_type=MESH,
        )

    across = there(z, 1 - x)

    @pl.loop(0, PARTS)
    def _(q):
        @pl.when(z > 0)
        def _():
            send_kin(view, q, ksend_own.at[0, q], there(z - 1, x)).start()

        @pl.when(z < 3)
        def _():
            send_kin(view, q, ksend_own.at[1, q], there(z + 1, x)).start()

        send_kin(view, q, ksend_x.at[0, q], across).start()

    count_copy = pltpu.make_async_remote_copy(
        src_ref=counts.at[core], dst_ref=counts.at[core], send_sem=count_sem.at[0], recv_sem=count_sem.at[1],
        device_id=other, device_id_type=MESH,
    )
    inputs[2].wait()
    inputs[3].wait()
    count_copy.start()
    for k in range(4):
        for side in (x, 1 - x):
            mat_copy(near[k] * 2 + side).start()
    curv_copy = pltpu.make_async_copy(curvature_ref, curv, curv_sem)
    curv_copy.start()

    for i in (1, 4, 5):
        inputs[i].wait()
    rows = lax.broadcasted_iota(jnp.int32, (frames, 1), 0)
    starts = jnp.zeros((frames, 1), jnp.int32)
    finish = jnp.zeros((frames, 1), jnp.int32)
    for f in range(frames):
        starts = jnp.where(rows == f, bounds_ref[f], starts)
        finish = jnp.where(rows == f, bounds_ref[f + 1], finish)
    seconds = lax.broadcasted_iota(jnp.int32, (frames, samples), 1)
    plasma = plasma_ref[...]
    inside = jnp.where((seconds >= starts) & (seconds < finish), plasma, 0.0)
    reaches = jnp.maximum(finish - jnp.maximum(seconds, starts), 0).astype(jnp.float32) * plasma
    length = (finish - starts).astype(jnp.float32)
    level = jnp.sum(inside, axis=1, keepdims=True) / length
    integral = jnp.sum(reaches, axis=1, keepdims=True) / (length * samples)

    def gate_row(slot, sub):
        first = (slot * 2 + core) * blocks
        lane = lax.broadcasted_iota(jnp.int32, (1, piece), 1) + (sub * piece - core * pad)
        row = jnp.full((1, piece), mask_ref[0, first], jnp.int32)
        for i in range(1, blocks):
            row = jnp.where(lane >= i * block, mask_ref[0, first + i], row)
        return row.astype(jnp.float32)

    def forward(slot, total, landed):
        mat_copy(slot).wait()

        def step(sub, total):
            cols = pl.ds(pl.multiple_of(sub * piece, 128), piece)
            gates = gate_row(slot, sub)
            slope = kin[slot, 0:1, cols] * gates
            inter = kin[slot, 1:2, cols] * gates
            images = (integral * slope + level * inter).astype(jnp.bfloat16)
            return total + lax.dot_general(
                images, mat[slot, :, cols], (((1,), (1,)), ((), ())), preferred_element_type=jnp.float32
            )

        for q in range(PARTS):
            if not landed:
                send_kin(slot, q, ksend_x.at[0, q], across).wait_recv()
            total = lax.fori_loop(q * each, (q + 1) * each, step, total)
        return total

    total = jnp.zeros((frames, bins), jnp.float32)
    total = forward(view, total, True)
    curv_copy.wait()
    for start in range(0, shard, piece):
        size = min(piece, shard - start)
        c = curv[:, start:start + size]
        cc = jnp.sum(c * (integral * integral), axis=0, keepdims=True)
        cp = jnp.sum(c * (integral * level), axis=0, keepdims=True)
        pp = jnp.sum(c * (level * level), axis=0, keepdims=True)
        scale = 1.0 / (cc * pp - cp * cp)
        coef[0:1, start:start + size] = cc * scale
        coef[1:2, start:start + size] = cp * scale
        coef[2:3, start:start + size] = pp * scale

    def relay(k, q, onward):
        slot = near[k] * 2 + x
        send_kin(slot, q, ksend_x.at[k, q], across).wait_recv()
        if onward is not None:
            send_kin(slot, q, ksend_z.at[k - 1, q], there(onward, x)).start()
        send_kin(slot, q, ksend_x.at[k, q], across).start()

    @pl.when(inner == 0)
    def _():
        for k in range(1, 4):

            @pl.loop(0, PARTS)
            def _(q):
                relay(k, q, None)

    @pl.when(inner == 1)
    def _():
        @pl.loop(0, PARTS)
        def _(q):
            relay(1, q, 3 - z)
            relay(2, q, 3 * (z // 2))

        @pl.loop(0, PARTS)
        def _(q):
            relay(3, q, 3 * (z // 2))

    for k in range(1, 4):
        total = forward(near[k] * 2 + x, total, True)
    for k in range(4):
        total = forward(near[k] * 2 + (1 - x), total, False)

    proj[core] = total
    proj_copy = pltpu.make_async_remote_copy(
        src_ref=proj.at[core], dst_ref=proj.at[core], send_sem=proj_sem.at[0], recv_sem=proj_sem.at[1],
        device_id=other, device_id_type=MESH,
    )
    proj_copy.start()
    count_copy.wait()
    proj_copy.wait()
    projection = proj[0] + proj[1]
    sinogram = jnp.concatenate([counts[0, 0], counts[1, 0]], axis=0)
    weight = jnp.concatenate([counts[0, 1], counts[1, 1]], axis=0)
    residual = rounded(weight * (sinogram - projection))
    slope_row = jnp.sum(integral * residual, axis=0, keepdims=True)
    inter_row = jnp.sum(level * residual, axis=0, keepdims=True)
    index = lax.broadcasted_iota(jnp.int32, (16, bins), 0)
    both = jnp.where(index % 2 == 0, slope_row, inter_row)
    high = rounded(both)
    middle = rounded(both - high)
    low = both - high - middle
    lhs[...] = jnp.where(
        index < 2, high, jnp.where(index < 4, middle, jnp.where(index < 6, low, 0.0))
    ).astype(jnp.bfloat16)

    def back(slot, sub):
        cols = pl.ds(pl.multiple_of(sub * piece, 128), piece)
        parts = jnp.dot(lhs[...], mat[slot, :, cols], preferred_element_type=jnp.float32)
        return (parts[0:2] + parts[2:4] + parts[4:6]) * gate_row(slot, sub), cols

    owners = near[::-1]

    sum_span = wide // SUM_PARTS
    sum_each = PIECES // SUM_PARTS

    def sum_part(q):
        return pl.ds(pl.multiple_of(q * sum_span, 128), sum_span)

    def xcopy(k, q):
        return pltpu.make_async_remote_copy(
            src_ref=xsend.at[k, :, sum_part(q)], dst_ref=xrecv.at[k, :, sum_part(q)],
            send_sem=xs_sem.at[k, q], recv_sem=xr_sem.at[k, q], device_id=across, device_id_type=MESH,
        )

    def zcopy(k, q):
        if k == 2:
            to, place = near[1], 4 + z % 2
        else:
            to = z + 1 - 2 * (z // 2)
            place = owners[0] if k == 0 else (1 - inner) * owners[1] + inner * (4 + z // 2)
        return pltpu.make_async_remote_copy(
            src_ref=zsend.at[k, :, sum_part(q)], dst_ref=zrecv.at[place, :, sum_part(q)],
            send_sem=zs_sem.at[k, q], recv_sem=zr_sem.at[place, q],
            device_id=there(to, x), device_id_type=MESH,
        )

    def arrived(place, q):
        pltpu.make_async_remote_copy(
            src_ref=zrecv.at[place, :, sum_part(q)], dst_ref=zrecv.at[place, :, sum_part(q)],
            send_sem=zs_sem.at[0, q], recv_sem=zr_sem.at[place, q], device_id=across, device_id_type=MESH,
        ).wait_recv()

    for k in range(4):

        @pl.loop(0, SUM_PARTS)
        def _(q):
            for i in range(sum_each):
                values, cols = back(owners[k] * 2 + 1 - x, q * sum_each + i)
                xsend[k, :, cols] = values
            xcopy(k, q).start()

    @pl.loop(0, PARTS)
    def _(q):
        for k in range(4):
            send_kin(near[k] * 2 + x, q, ksend_x.at[k, q], across).wait_send()

        @pl.when(inner == 1)
        def _():
            for k in range(1, 4):
                send_kin(near[k] * 2 + x, q, ksend_z.at[k - 1, q], across).wait_send()

        @pl.when(z > 0)
        def _():
            send_kin(view, q, ksend_own.at[0, q], across).wait_send()

        @pl.when(z < 3)
        def _():
            send_kin(view, q, ksend_own.at[1, q], across).wait_send()

    for k in range(4):

        @pl.loop(0, SUM_PARTS)
        def _(q):
            for i in range(sum_each):
                values, cols = back(owners[k] * 2 + x, q * sum_each + i)
                zsend[k, :, cols] = values
            cols = sum_part(q)
            xcopy(k, q).wait_recv()

            @pl.when(inner == 1)
            def _():
                places = (owners[k],) if k < 3 else (4, 5)
                rest = xrecv[k, :, cols]
                for place in places:
                    arrived(place, q)
                    rest = rest + zrecv[place, :, cols]
                zsend[k, :, cols] = zsend[k, :, cols] + rest

            @pl.when(inner == 0)
            def _():
                rest = xrecv[k, :, cols]
                if k == 3:
                    arrived(5 - z // 2, q)
                    rest = rest + zrecv[5 - z // 2, :, cols]
                zsend[k, :, cols] = zsend[k, :, cols] + rest

            if k < 3:
                zcopy(k, q).start()

    def finish_with(shift):
        slope = zsend[3, 0:1, shift:shift + shard]
        inter = zsend[3, 1:2, shift:shift + shard]
        cc, cp, pp = coef[0:1], coef[1:2], coef[2:3]
        out_ref[0:1] = kinetic_ref[0:1] + (pp * slope - cp * inter)
        out_ref[1:2] = kinetic_ref[1:2] + (cc * inter - cp * slope)

    @pl.when(core == 0)
    def _():
        finish_with(0)

    @pl.when(core == 1)
    def _():
        finish_with(pad)

    @pl.loop(0, SUM_PARTS)
    def _(q):
        for k in range(4):
            xcopy(k, q).wait_send()
        for k in range(3):
            zcopy(k, q).wait_send()


def fused(sinogram, stat_weight, projector, block_mask, kinetic, curvature, plasma, bounds):
    shard = kinetic.shape[1]
    frames = curvature.shape[0]
    bins = projector.shape[0]
    wide = padded_width(shard)
    dma = pltpu.SemaphoreType.DMA
    vmem = pl.BlockSpec(memory_space=pltpu.VMEM)
    hbm = pl.BlockSpec(memory_space=pl.ANY)
    f32 = jnp.float32
    return pl.pallas_call(
        kernel,
        out_shape=jax.ShapeDtypeStruct(kinetic.shape, f32),
        in_specs=[hbm] * 8,
        out_specs=vmem,
        scratch_shapes=[
            pltpu.VMEM(kinetic.shape, f32),
            pltpu.VMEM((1,) + plasma.shape, f32),
            pltpu.SMEM(bounds.shape, jnp.int32),
            pltpu.SMEM(block_mask.shape, jnp.int32),
            dma((6,)),
            pltpu.VMEM((8, 2, wide), f32),
            pltpu.VMEM((8, bins, wide), jnp.bfloat16),
            pltpu.VMEM((frames, shard), f32),
            pltpu.VMEM((3, shard), f32),
            pltpu.VMEM((2, 2) + sinogram.shape, f32),
            pltpu.VMEM((2, frames, bins), f32),
            pltpu.VMEM((4, 2, wide), f32),
            pltpu.VMEM((4, 2, wide), f32),
            pltpu.VMEM((4, 2, wide), f32),
            pltpu.VMEM((6, 2, wide), f32),
            pltpu.VMEM((16, bins), jnp.bfloat16),
            dma((8,)),
            dma,
            dma((4, PARTS)),
            dma((3, PARTS)),
            dma((2, PARTS)),
            dma((8, PARTS)),
            dma((2,)),
            dma((2,)),
            dma((4, SUM_PARTS)),
            dma((4, SUM_PARTS)),
            dma((3, SUM_PARTS)),
            dma((6, SUM_PARTS)),
        ],
        compiler_params=pltpu.CompilerParams(
            collective_id=0, has_side_effects=True, vmem_limit_bytes=56 * 2**20
        ),
        cost_estimate=pl.CostEstimate(
            flops=2 * frames * projector.size, bytes_accessed=projector.size, transcendentals=0
        ),
    )(kinetic, plasma, sinogram, stat_weight, bounds, block_mask, projector, curvature)


def padded_width(shard):
    step = 128 * PIECES
    return -(-shard // step) * step


def fits(mesh, projector, block_mask, kinetic, sinogram):
    shard = kinetic.shape[1]
    return (
        mesh.shape["view"] == 8
        and mesh.shape["frame"] == 2
        and 2 * shard % 128 == 0
        and padded_width(shard) <= 2 * shard
        and block_mask.shape[1] % 16 == 0
        and projector.shape == (16, 16 * shard)
        and sinogram.shape == (8, 16)
    )


def solution(mesh):
    in_specs = (
        P(("grp", "frame"), "view"),
        P(("grp", "frame"), "view"),
        P("view", None),
        P("view", None),
        P(None, ("grp", "view", "frame")),
        P(None, ("grp", "view", "frame")),
        P("grp"),
        P("grp"),
    )
    out_specs = P(None, ("grp", "view", "frame"))

    def local(sinogram, stat_weight, projector, block_mask, kinetic, curvature, plasma, bounds):
        form = fused if fits(mesh, projector, block_mask, kinetic, sinogram) else plain
        return form(sinogram, stat_weight, projector, block_mask, kinetic, curvature, plasma, bounds)

    return jax.shard_map(local, mesh=mesh, in_specs=in_specs, out_specs=out_specs, check_vma=False)
```
